32 devices in a mesh: groups: 2 (over y), expert: 16 (over z, x, core).
Axes of the slice: x: 2, y: 2, z: 4, core: 2. Of those that a mesh axis runs over, the one named last changes fastest.
Arguments:
- tokens: bfloat16 [4096, 3584], P(('groups', 'expert')), parts along dimension 0, may hold values from -6 to 6
- gates: float32 [4096, 1], P(('groups', 'expert')), parts along dimension 0, may hold values from 0.1 to 1
- routes: int32 [4096, 1], P(('groups', 'expert')), parts along dimension 0, may hold values from 0 to 1; in each aligned block of 128 rows (0 to 127, 128 to 255, ...) at most 96 rows name the same one
- counts: int32 [32], P(('groups', 'expert')), parts along dimension 0, may hold values from 64 to 128, as said below
- w_gate: bfloat16 [16, 1792, 256], P('expert'), may hold values from -0.09375 to 0.09375
- w_up: bfloat16 [16, 1792, 256], P('expert'), may hold values from -0.09375 to 0.09375
- w_down: bfloat16 [16, 256, 1792], P('expert'), may hold values from -0.1875 to 0.1875
- cotangent: bfloat16 [4096, 3584], P(('groups', 'expert')), parts along dimension 0, may hold values from -6 to 6
Outputs:
- mixed: bfloat16 [4096, 3584], P(('groups', 'expert')), parts along dimension 0
- grad_tokens: bfloat16 [4096, 3584], P(('groups', 'expert')), parts along dimension 0
- grad_gates: float32 [4096, 1], P(('groups', 'expert')), parts along dimension 0
- grad_w_gate: bfloat16 [32, 1792, 256], P(('groups', 'expert')), parts along dimension 0
- grad_w_up: bfloat16 [32, 1792, 256], P(('groups', 'expert')), parts along dimension 0
- grad_w_down: bfloat16 [32, 256, 1792], P(('groups', 'expert')), parts along dimension 0
The draws below stay inside these ranges and needn't reach their ends.
There are 2 independent parts, one for each index of `groups`. The reference program is written for one: setup_inputs(seed, part) draws one part's arguments, and reference() takes and returns one part's arrays. A program takes and returns all parts, laid end to end along the dimension named above; an argument that names none is the same for every part. Nothing has to cross between parts.
Inputs may be any that keep to these rules, and one draw needn't show every extreme that they name: `routes`: among the 128 rows of one device, no expert is named in more than 96 pairs, and some expert is named in exactly 96 pairs. `counts`: in every draw some device has all 128 slots live.
All inputs are finite; a program needn't handle non-finite values.
Results may differ from the reference program's by a relative error of at most 0.015.
Values may be sent and summed in bfloat16 or wider, within the bound.
A program may use at most 128 MiB of HBM per device.

```python
import math
import jax
import jax.numpy as jnp
import numpy as np
from jax import lax

D = 3584
FF = 1024
TOPK = 1
TOK_DEV = 128
EXPERTS = 2
DH = 1792
FQ = 256
CAP = 96
TOKENS = 2048
N_EXPERT = 16


def draw_counts(key, part):
    key = jax.random.fold_in(key, 7)
    first, second = jax.random.split(key)
    values = jax.random.randint(first, (N_EXPERT,), TOK_DEV // 2, TOK_DEV + 1)
    full_at = jax.random.randint(second, (), 0, N_EXPERT)
    return jnp.where(jnp.arange(N_EXPERT) == full_at, TOK_DEV, values).astype(jnp.int32)


def block_levels(rng, dims, pieces, low, high):
    def one(position, parts):
        heights = jax.random.uniform(jax.random.fold_in(jax.random.fold_in(rng, 6), position), (parts,), jnp.float32, low / len(pieces), high / len(pieces))
        return jnp.repeat(jnp.exp(heights), dims[position] // parts).reshape((-1,) + (1,) * (len(dims) - position - 1))

    level = one(*pieces[0])
    for cut in pieces[1:]:
        level = level * one(*cut)
    return level


def routed_block(key, own, number, rows, count, top, limit, slope):
    sequence = jax.random.permutation(key, count)
    packed, usual = portions_of(count, rows * top, limit, slope, True), portions_of(count, rows * top, limit, slope, False)
    places = jnp.arange(count)

    def named(tallies, turn):
        used = int((tallies > 0).sum())
        fixed = max(1, used // 4)
        shifted = fixed + (places - fixed + turn * (used - fixed)) % max(1, count - fixed)
        return jnp.zeros((count,), jnp.int32).at[sequence[jnp.where(places < fixed, places, shifted)]].set(jnp.asarray(tallies, jnp.int32))

    tallies = jnp.where(number % 4 == 0, named(packed, number // 4), named(usual, number - number // 4 - 1))
    mixed = jax.random.permutation(jax.random.fold_in(own, 3), count)
    giver, sink = mixed[0:count // 2 * 2:2], mixed[1:count // 2 * 2:2]
    slack = jnp.minimum(tallies[giver] - 1, limit - tallies[sink]) // 2
    slack = jnp.where((giver == sequence[0]) | (sink == sequence[0]) | (tallies[sink] == 0), 0, jnp.maximum(slack, 0))
    shifted = jax.random.randint(jax.random.fold_in(own, 4), (count // 2,), 0, 1 << 20) % (slack + 1)
    tallies = tallies.at[giver].add(-shifted).at[sink].add(shifted)
    members = jnp.searchsorted(jnp.cumsum(tallies), jnp.arange(rows * top), side="right").astype(jnp.int32)
    listing = members.reshape(top, rows).T
    listing = listing[jax.random.permutation(jax.random.fold_in(own, 1), rows)]
    turn = jax.random.randint(jax.random.fold_in(own, 2), (rows, 1), 0, top)
    return jnp.take_along_axis(listing, (jnp.arange(top)[None, :] + turn) % top, axis=1)


def portions_of(count, total, most, slope, full):
    weights = [(1 << 20) // math.isqrt(standing ** slope) + 1 for standing in range(1, count + 1)]
    largest = most if full else min(most, max(-(-total // count), total * weights[0] // sum(weights)))
    least = 1 if total - largest >= count - 1 else 0
    given, rest = [largest] + [least] * (count - 1), total - largest - least * (count - 1)
    while rest > 0:
        movable = [i for i in range(1, count) if given[i] < largest] or [i for i in range(1, count) if given[i] < most]
        pool, remaining = sum([weights[i] for i in movable]), rest
        for i in movable:
            addition = min(most - given[i], max(1, remaining * weights[i] // pool), rest)
            given[i] = given[i] + addition
            rest = rest - addition
    return np.array(given)


def noise(own_key, dims, scale, reach, shards=(), held_as=jnp.bfloat16):
    gain = block_levels(own_key, dims, shards, -0.22, 0.18) if shards else 1.0
    result = jax.random.normal(own_key, dims, jnp.float32) * scale * gain
    return jnp.minimum(jnp.maximum(result, -reach), reach).astype(held_as)


def setup_inputs(seed: int = 0, part: int = 0) -> dict:
    streams_of = jax.random.split(jax.random.key(seed), 9)
    part_keys = jax.random.split(jax.random.fold_in(streams_of[8], part), 9)
    tokens = noise(part_keys[0], (TOKENS, D), 1.0, 6.0, ((0, 16),))
    gates = jnp.clip(0.1 + 0.9 * jax.random.uniform(part_keys[1], (TOKENS, TOPK), jnp.float32) ** block_levels(part_keys[1], (TOKENS, TOPK), ((0, 16),), -0.2, 0.2), 0.1, 1.0)
    routes_keys = jax.random.split(jax.random.fold_in(part_keys[2], 1), TOKENS // TOK_DEV)
    routes_turns = jax.random.permutation(jax.random.fold_in(part_keys[2], 3), TOKENS // TOK_DEV)
    routes = jax.vmap(lambda own, number: routed_block(jax.random.fold_in(part_keys[2], 2), own, number, TOK_DEV, EXPERTS, TOPK, CAP, 2))(routes_keys, routes_turns).reshape((TOKENS, TOPK))
    counts = draw_counts(jax.random.fold_in(jax.random.fold_in(streams_of[8], part), 71), part)
    w_gate = noise(streams_of[4], (N_EXPERT, DH, FQ), D ** -0.5, 0.09375, ((0, 16),))
    w_up = noise(streams_of[5], (N_EXPERT, DH, FQ), D ** -0.5, 0.09375, ((0, 16),))
    w_down = noise(streams_of[6], (N_EXPERT, FQ, DH), FF ** -0.5, 0.1875, ((0, 16),))
    cotangent = noise(part_keys[7], (TOKENS, D), 1.0, 6.0, ((0, 16),))
    return {"tokens": tokens, "gates": gates, "routes": routes, "counts": counts, "w_gate": w_gate, "w_up": w_up, "w_down": w_down, "cotangent": cotangent}


def expert_rows(rows, scaled, wg_full, wu_full, wd_full, wg_parts, wu_parts, wd_parts):
    count = rows.shape[0]
    g = jnp.dot(rows, wg_full, preferred_element_type=jnp.float32)
    u = jnp.dot(rows, wu_full, preferred_element_type=jnp.float32)
    sg = jax.nn.sigmoid(g)
    act = (g * sg * u).astype(jnp.bfloat16)
    act_parts = act.reshape(count, 4, FQ).astype(jnp.float32)
    out_parts = jnp.einsum("nbf,bfd->nbd", act_parts, wd_parts.astype(jnp.float32), precision=lax.Precision.HIGHEST).astype(jnp.bfloat16)
    out_parts = lax.optimization_barrier(out_parts)
    out = jnp.sum(out_parts.astype(jnp.float32), axis=1).astype(jnp.bfloat16)
    d_act = jnp.dot(scaled, wd_full.T, preferred_element_type=jnp.float32)
    grad_wd = jnp.dot(act.T, scaled, preferred_element_type=jnp.float32)
    d_gate = (d_act * u * sg * (1.0 + g * (1.0 - sg))).astype(jnp.bfloat16)
    d_up = (d_act * g * sg).astype(jnp.bfloat16)
    grad_wg = jnp.dot(rows.T, d_gate, preferred_element_type=jnp.float32)
    grad_wu = jnp.dot(rows.T, d_up, preferred_element_type=jnp.float32)
    gate_parts = d_gate.reshape(count, 4, FQ).astype(jnp.float32)
    up_parts = d_up.reshape(count, 4, FQ).astype(jnp.float32)
    row_parts = jnp.einsum("nbf,bdf->nbd", gate_parts, wg_parts.astype(jnp.float32), precision=lax.Precision.HIGHEST)
    row_parts = row_parts + jnp.einsum("nbf,bdf->nbd", up_parts, wu_parts.astype(jnp.float32), precision=lax.Precision.HIGHEST)
    row_parts = lax.optimization_barrier(row_parts.astype(jnp.bfloat16))
    d_row = jnp.sum(row_parts.astype(jnp.float32), axis=1).astype(jnp.bfloat16)
    return out, d_row, grad_wg, grad_wu, grad_wd


def reference(tokens, gates, routes, counts, w_gate, w_up, w_down, cotangent):
    peers = N_EXPERT
    flat_n = TOKENS * TOPK
    row_ids = jnp.arange(TOKENS, dtype=jnp.int32)
    source = row_ids // TOK_DEV
    valid = (row_ids % TOK_DEV) < counts[source]
    target = jnp.where(valid[:, None], routes, EXPERTS).astype(jnp.int32).reshape(peers, TOK_DEV * TOPK)
    onehot = (target[:, :, None] == jnp.arange(EXPERTS, dtype=jnp.int32)[None, None, :]).astype(jnp.int32)
    running = jnp.cumsum(onehot, axis=1)
    slot_pos = jnp.sum((running - 1) * onehot, axis=2).astype(jnp.int32)
    flat_target = target.reshape(flat_n)
    flat_source = jnp.repeat(jnp.arange(peers, dtype=jnp.int32), TOK_DEV * TOPK)
    slot = flat_source * CAP + slot_pos.reshape(flat_n)
    table = jnp.full((EXPERTS, peers * CAP), flat_n, jnp.int32)
    table = table.at[flat_target, slot].set(jnp.arange(flat_n, dtype=jnp.int32), mode="drop")
    tok_ext = jnp.concatenate([tokens, jnp.zeros((1, D), tokens.dtype)], axis=0)
    cot_ext = jnp.concatenate([cotangent, jnp.zeros((1, D), cotangent.dtype)], axis=0)
    gate_ext = jnp.concatenate([gates.reshape(flat_n), jnp.zeros((1,), gates.dtype)], axis=0)
    wg_blocks = w_gate.reshape(EXPERTS, 4, 2, DH, FQ)
    wu_blocks = w_up.reshape(EXPERTS, 4, 2, DH, FQ)
    wd_blocks = w_down.reshape(EXPERTS, 4, 2, FQ, DH)

    def step(carry, items):
        mixed_acc, dx_acc, dg_acc = carry
        wg, wu, wd, ids = items
        wg_full = wg.transpose(1, 2, 0, 3).reshape(D, FF)
        wu_full = wu.transpose(1, 2, 0, 3).reshape(D, FF)
        wd_parts = wd.transpose(0, 2, 1, 3).reshape(4, FQ, D)
        wd_full = wd_parts.reshape(FF, D)
        wg_parts = wg.reshape(4, D, FQ)
        wu_parts = wu.reshape(4, D, FQ)
        rows_at = jnp.where(ids < flat_n, ids // TOPK, TOKENS).astype(jnp.int32)
        rows = tok_ext[rows_at]
        cot_rows = cot_ext[rows_at].astype(jnp.float32)
        gate_rows = gate_ext[ids]
        scaled = (gate_rows[:, None] * cot_rows).astype(jnp.bfloat16)
        out, d_row, grad_wg, grad_wu, grad_wd = expert_rows(rows, scaled, wg_full, wu_full, wd_full, wg_parts, wu_parts, wd_parts)
        out32 = out.astype(jnp.float32)
        mixed_acc = mixed_acc.at[rows_at].add(gate_rows[:, None] * out32)
        dx_acc = dx_acc.at[rows_at].add(d_row.astype(jnp.float32))
        dg_acc = dg_acc.at[ids].add(jnp.sum(cot_rows * out32, axis=1))
        grad_wg = grad_wg.astype(jnp.bfloat16).reshape(2, DH, 4, FQ).transpose(2, 0, 1, 3)
        grad_wu = grad_wu.astype(jnp.bfloat16).reshape(2, DH, 4, FQ).transpose(2, 0, 1, 3)
        grad_wd = grad_wd.astype(jnp.bfloat16).reshape(4, FQ, 2, DH).transpose(0, 2, 1, 3)
        return (mixed_acc, dx_acc, dg_acc), (grad_wg, grad_wu, grad_wd)

    start = (jnp.zeros((TOKENS + 1, D), jnp.float32), jnp.zeros((TOKENS + 1, D), jnp.float32), jnp.zeros((flat_n + 1,), jnp.float32))
    (mixed_acc, dx_acc, dg_acc), (grad_wg, grad_wu, grad_wd) = lax.scan(step, start, (wg_blocks, wu_blocks, wd_blocks, table))
    mixed = mixed_acc[:TOKENS].astype(jnp.bfloat16)
    grad_tokens = dx_acc[:TOKENS].astype(jnp.bfloat16)
    grad_gates = dg_acc[:flat_n].reshape(TOKENS, TOPK)
    grad_wg = grad_wg.reshape(N_EXPERT, DH, FQ)
    grad_wu = grad_wu.reshape(N_EXPERT, DH, FQ)
    grad_wd = grad_wd.reshape(N_EXPERT, FQ, DH)
    return mixed, grad_tokens, grad_gates, grad_wg, grad_wu, grad_wd
```

```python
import jax
import jax.numpy as jnp
from jax import lax
from jax.sharding import PartitionSpec as P

BF16 = jnp.bfloat16
F32 = jnp.float32


def swap(value, mask):
    pairs = [(source, source ^ mask) for source in range(lax.axis_size("expert"))]
    return lax.ppermute(value, "expert", pairs)


def dot(a, b, ca, cb):
    return lax.dot_general(a, b, (((ca,), (cb,)), ((), ())), preferred_element_type=F32)


def on_device(tokens, gates, routes, counts, w_gate, w_up, w_down, cotangent):
    peers = lax.axis_size("expert")
    tok_rows, topk = routes.shape
    width = tokens.shape[1]
    half = width // 2
    quarter = w_gate.shape[2]
    experts = peers // 8
    capacity = max(2, 3 * tok_rows * topk // (2 * experts))
    flat_n = tok_rows * topk
    slots = experts * capacity
    me = lax.axis_index("expert")
    mine, core = me // 8, me % 2

    gate_up = jnp.concatenate([w_gate[0], w_up[0]], axis=1)
    down = w_down[0]
    gate_up_z = swap(gate_up, 4)
    down_z = swap(down, 4)

    valid = jnp.arange(tok_rows, dtype=jnp.int32) < counts[0]
    target = jnp.where(valid[:, None], routes, experts).reshape(flat_n)
    onehot = (target[:, None] == jnp.arange(experts, dtype=jnp.int32)[None, :]).astype(F32)
    earlier = (
        jnp.arange(flat_n)[:, None] > jnp.arange(flat_n)[None, :]
    ).astype(BF16)
    before = dot(earlier, onehot.astype(BF16), 1, 0)
    slot_pos = jnp.sum(before * onehot, axis=1).astype(jnp.int32)
    place = jnp.where(target < experts, (target ^ mine) * capacity + slot_pos, slots)
    put = (place[:, None] == jnp.arange(slots, dtype=jnp.int32)[None, :]).astype(BF16)
    gate_flat = gates.reshape(flat_n)
    if topk == 1:
        tok_flat, cot_flat = tokens, cotangent
    else:
        tok_flat = jnp.repeat(tokens, topk, axis=0)
        cot_flat = jnp.repeat(cotangent, topk, axis=0)
    cot_rows = cot_flat.astype(F32)
    scaled = (gate_flat[:, None] * cot_rows).astype(BF16)

    def own_first(rows):
        return jnp.where(
            core == 0, rows, jnp.concatenate([rows[:, half:], rows[:, :half]], axis=1)
        )

    packed_x = dot(put, own_first(tok_flat), 0, 0).astype(BF16)
    packed_s = dot(put, own_first(scaled), 0, 0).astype(BF16)

    def dispatch(packed):
        here = packed[:capacity]
        others = jnp.concatenate(
            [
                swap(packed[d * capacity : (d + 1) * capacity], 8 * d)
                for d in range(1, experts)
            ],
            axis=0,
        )
        return jnp.concatenate([here, others, swap(here, 2), swap(others, 2)], axis=0)

    rows = dispatch(packed_x)
    grads = dispatch(packed_s)

    gate_up_c, down_c = swap(gate_up, 1), swap(down, 1)
    gate_up_zc, down_zc = swap(gate_up_z, 1), swap(down_z, 1)
    w_in = jnp.concatenate(
        [
            jnp.concatenate([gate_up, gate_up_z], axis=1),
            jnp.concatenate([gate_up_c, gate_up_zc], axis=1),
        ],
        axis=0,
    )
    w_out = jnp.concatenate(
        [
            jnp.concatenate([down, down_c], axis=1),
            jnp.concatenate([down_z, down_zc], axis=1),
        ],
        axis=0,
    )

    pre = dot(rows, w_in, 1, 0)
    g = jnp.concatenate([pre[:, :quarter], pre[:, 2 * quarter : 3 * quarter]], axis=1)
    u = jnp.concatenate([pre[:, quarter : 2 * quarter], pre[:, 3 * quarter :]], axis=1)
    sg = jax.nn.sigmoid(g)
    act = (g * sg * u).astype(BF16)

    def give_back(part):
        ready = part[:slots] + swap(part[slots:].astype(BF16), 2).astype(F32)
        ready = ready.astype(BF16)
        return jnp.concatenate(
            [ready[:capacity]]
            + [
                swap(ready[d * capacity : (d + 1) * capacity], 8 * d)
                for d in range(1, experts)
            ],
            axis=0,
        )

    back_out = give_back(dot(act, w_out, 1, 0))
    d_act = dot(grads, w_out, 1, 1)
    d_gate = (d_act * u * sg * (1.0 + g * (1.0 - sg))).astype(BF16)
    d_up = (d_act * g * sg).astype(BF16)
    d_pre = jnp.concatenate(
        [d_gate[:, :quarter], d_up[:, :quarter], d_gate[:, quarter:], d_up[:, quarter:]], axis=1
    )
    back_dx = give_back(dot(d_pre, w_in, 1, 1))

    in_theirs = dot(rows[:, half:], d_pre, 0, 0).astype(BF16)
    out_theirs = dot(act, grads[:, half:], 0, 0).astype(BF16)
    in_mine = dot(rows[:, :half], d_pre, 0, 0) + swap(in_theirs, 1).astype(F32)
    out_mine = dot(act, grads[:, :half], 0, 0) + swap(out_theirs, 1).astype(F32)
    in_sum = in_mine[:, : 2 * quarter] + swap(
        in_mine[:, 2 * quarter :].astype(BF16), 4
    ).astype(F32)
    out_sum = out_mine[:quarter] + swap(out_mine[quarter:].astype(BF16), 4).astype(F32)
    grad_in = in_sum.astype(BF16)
    grad_wd = out_sum.astype(BF16)

    out_rows = own_first(dot(put, back_out, 1, 0))
    dx_rows = own_first(dot(put, back_dx, 1, 0))
    mixed = jnp.sum(
        (gate_flat[:, None] * out_rows).reshape(tok_rows, topk, width), axis=1
    ).astype(BF16)
    grad_tokens = jnp.sum(dx_rows.reshape(tok_rows, topk, width), axis=1).astype(BF16)
    grad_gates = jnp.sum(cot_rows * out_rows, axis=1).reshape(tok_rows, topk)
    return (
        mixed,
        grad_tokens,
        grad_gates,
        grad_in[:, :quarter][None],
        grad_in[:, quarter:][None],
        grad_wd[None],
    )


def solution(mesh):
    both, rows = ("groups", "expert"), P(("groups", "expert"), None)
    block = P(both, None, None)
    weight = P("expert", None, None)
    return jax.shard_map(
        on_device,
        mesh=mesh,
        in_specs=(rows, rows, rows, P(both), weight, weight, weight, rows),
        out_specs=(rows, rows, rows, block, block, block),
        check_vma=False,
    )
```

```python
import functools

import jax
import jax.numpy as jnp
from jax import lax
from jax.experimental import pallas as pl
from jax.experimental.pallas import tpu as pltpu
from jax.sharding import PartitionSpec as P

BF16 = jnp.bfloat16
F32 = jnp.float32


def swap(value, mask):
    pairs = [(source, source ^ mask) for source in range(lax.axis_size("expert"))]
    return lax.ppermute(value, "expert", pairs)


def dot(a, b, ca, cb):
    return lax.dot_general(a, b, (((ca,), (cb,)), ((), ())), preferred_element_type=F32)


def layer_kernel(
    cap, half, quarter,
    px, ps, wg, wu, wd,
    bo, bx, og, ou, od,
    rows, grads, gates_w, ups_w, downs_w, g_buf, u_buf, act, dd,
    out_keep, out_send, out_recv, dx_keep, dx_send, dx_recv,
    tg, tu, td, rg, ru, rd, zsg, zsu, zsd, zrg, zru, zrd,
    send_sem, recv_sem, local_sem,
):
    me, group = lax.axis_index("expert"), lax.axis_index("groups")
    slots = 2 * cap
    step = cap // 2

    def partner(mask):
        return me + mask - 2 * mask * lax.rem(me // mask, 2)

    core, near, far, home = (
        {"expert": partner(1)}, {"expert": partner(2)}, {"expert": partner(4)},
        {"expert": partner(8)},
    )
    twin = {"groups": 1 - group}
    barrier = pltpu.get_barrier_semaphore()
    for other in (core, near, far, home, twin):
        pl.semaphore_signal(barrier, inc=1, device_id=other, device_id_type=pl.DeviceIdType.MESH)
    pl.semaphore_wait(barrier, 5)

    sent = []

    def send(src, dst, to):
        number = len(sent)
        copy = pltpu.make_async_remote_copy(
            src_ref=src, dst_ref=dst, send_sem=send_sem.at[number],
            recv_sem=recv_sem.at[number], device_id=to,
            device_id_type=pl.DeviceIdType.MESH,
        )
        copy.start()
        sent.append(copy)
        return copy

    locals_ = []

    def local(src, dst):
        copy = pltpu.make_async_copy(src, dst, local_sem.at[len(locals_)])
        copy.start()
        locals_.append(copy)
        return copy

    def part(ref, start, size):
        return ref.at[pl.ds(start, size)]

    over_x = [
        send(part(px, cap + i * step, step), part(rows, cap + i * step, step), home)
        for i in range(2)
    ]
    over_s = [
        send(part(ps, cap + i * step, step), part(grads, cap + i * step, step), home)
        for i in range(2)
    ]
    near_x = [send(part(px, 0, cap), part(rows, slots, cap), near)]
    near_s = [send(part(ps, 0, cap), part(grads, slots, cap), near)]
    weights = ((wg, gates_w), (wu, ups_w), (wd, downs_w))

    def group_half(ref, which):
        size = ref.shape[0] // 2
        return ref.at[pl.ds(pl.multiple_of(which * size, size), size)]

    far_w = [send(group_half(w, group), group_half(b.at[2], group), far) for w, b in weights]
    core_w = [send(w, b.at[1], core) for w, b in weights]
    own_w = [local(w, b.at[0]) for w, b in weights]
    own_r = [local(part(px, 0, cap), part(rows, 0, cap)),
             local(part(ps, 0, cap), part(grads, 0, cap))]

    for i in range(2):
        over_x[i].wait_recv()
        block = part(rows, cap + i * step, step)
        near_x.append(send(block, part(rows, slots + cap + i * step, step), near))
    twin_w = []
    for i, (w, b) in enumerate(weights):
        far_w[i].wait_recv()
        twin_w.append(send(group_half(b.at[2], group), group_half(b.at[2], group), twin))
    far_core_w = []
    for i, (w, b) in enumerate(weights):
        twin_w[i].wait_recv()
        far_core_w.append(send(b.at[2], b.at[3], core))
    for i in range(2):
        over_s[i].wait_recv()
        block = part(grads, cap + i * step, step)
        near_s.append(send(block, part(grads, slots + cap + i * step, step), near))

    for copy in own_w + own_r:
        copy.wait()
    for copy in near_x + core_w + far_core_w:
        copy.wait_recv()

    for q in range(2):
        columns = slice(q * quarter, (q + 1) * quarter)
        left, right = rows[:, :half], rows[:, half:]
        g = dot(left, gates_w[2 * q], 1, 0) + dot(right, gates_w[2 * q + 1], 1, 0)
        u = dot(left, ups_w[2 * q], 1, 0) + dot(right, ups_w[2 * q + 1], 1, 0)
        g_buf[:, columns] = g
        u_buf[:, columns] = u
        act[:, columns] = (g * jax.nn.sigmoid(g) * u).astype(BF16)

    tile = half // 2

    def give(keep, away, arrived, make):
        for h in range(2):
            @pl.loop(0, 2)
            def _(t):
                at = pl.multiple_of(t * tile, tile)
                value = make(h, pl.ds(at, tile)).astype(BF16)
                columns = pl.ds(pl.multiple_of(h * half + t * tile, tile), tile)
                keep[:, columns] = value[:slots]
                away[:, columns] = value[slots:]
        return [
            send(part(away, at, step), part(arrived, at, step), near)
            for at in (cap, cap + step, 0, step)
        ]

    def make_out(h, columns):
        return dot(act[:, :quarter], downs_w[h, :, columns], 1, 0) + dot(
            act[:, quarter:], downs_w[2 + h, :, columns], 1, 0
        )

    near_out = give(out_keep, out_send, out_recv, make_out)

    for copy in near_s:
        copy.wait_recv()
    for q in range(2):
        columns = slice(q * quarter, (q + 1) * quarter)
        d_act = dot(grads[:, :half], downs_w[2 * q], 1, 1) + dot(
            grads[:, half:], downs_w[2 * q + 1], 1, 1
        )
        g, u = g_buf[:, columns], u_buf[:, columns]
        sg = jax.nn.sigmoid(g)
        dd[:, columns] = (d_act * u * sg * (1.0 + g * (1.0 - sg))).astype(BF16)
        dd[:, slice((2 + q) * quarter, (3 + q) * quarter)] = (d_act * g * sg).astype(BF16)

    @pl.loop(0, 2)
    def _(t):
        at = pl.multiple_of(t * tile, tile)
        value = dot(act[...], grads[:, pl.ds(pl.multiple_of(half + at, tile), tile)], 0, 0)
        value = value.astype(BF16)
        td[0, :, pl.ds(at, tile)] = value[:quarter]
        td[1, :, pl.ds(at, tile)] = value[quarter:]

    core_d = [send(td.at[q], rd.at[q], core) for q in (1, 0)]
    width_step = 256

    @pl.loop(0, half // width_step)
    def _(t):
        at = pl.multiple_of(t * width_step, width_step)
        value = dot(rows[:, pl.ds(pl.multiple_of(half + at, width_step), width_step)], dd[...], 0, 0)
        value = value.astype(BF16)
        for q in range(2):
            tg[q, pl.ds(at, width_step)] = value[:, q * quarter : (q + 1) * quarter]
            tu[q, pl.ds(at, width_step)] = value[:, (2 + q) * quarter : (3 + q) * quarter]

    core_g = [send(tg.at[q], rg.at[q], core) for q in (1, 0)]
    core_u = [send(tu.at[q], ru.at[q], core) for q in (1, 0)]

    for copy in core_d:
        copy.wait_recv()

    @pl.loop(0, 2)
    def _(t):
        at = pl.multiple_of(t * tile, tile)
        value = dot(act[...], grads[:, pl.ds(at, tile)], 0, 0)
        od[:, pl.ds(at, tile)] = (value[:quarter] + rd[0, :, pl.ds(at, tile)].astype(F32)).astype(BF16)
        zsd[:, pl.ds(at, tile)] = (value[quarter:] + rd[1, :, pl.ds(at, tile)].astype(F32)).astype(BF16)

    far_d = send(zsd, zrd, far)

    for copy in core_g + core_u:
        copy.wait_recv()

    @pl.loop(0, half // width_step)
    def _(t):
        at = pl.ds(pl.multiple_of(t * width_step, width_step), width_step)
        value = dot(rows[:, at], dd[...], 0, 0)
        for column, got, mine, away in ((0, rg, og, zsg), (2, ru, ou, zsu)):
            first = value[:, column * quarter : (column + 1) * quarter]
            second = value[:, (column + 1) * quarter : (column + 2) * quarter]
            mine[at] = (first + got[0, at].astype(F32)).astype(BF16)
            away[at] = (second + got[1, at].astype(F32)).astype(BF16)

    far_g = send(zsg, zrg, far)
    far_u = send(zsu, zru, far)

    def make_dx(h, columns):
        value = dot(dd[:, :quarter], gates_w[h, columns], 1, 1)
        value = value + dot(dd[:, quarter : 2 * quarter], gates_w[2 + h, columns], 1, 1)
        value = value + dot(dd[:, 2 * quarter : 3 * quarter], ups_w[h, columns], 1, 1)
        return value + dot(dd[:, 3 * quarter :], ups_w[2 + h, columns], 1, 1)

    near_dx = give(dx_keep, dx_send, dx_recv, make_dx)

    homeward = []
    for keep, arrived, copies, result in (
        (out_keep, out_recv, near_out, bo), (dx_keep, dx_recv, near_dx, bx),
    ):
        for copy, at in zip(copies, (cap, cap + step, 0, step)):
            copy.wait_recv()
            total = keep[at : at + step].astype(F32) + arrived[at : at + step].astype(F32)
            keep[at : at + step] = total.astype(BF16)
            if at >= cap:
                homeward.append(send(part(keep, at, step), part(result, at, step), home))
            else:
                local(part(keep, at, step), part(result, at, step))

    for copy, mine, got in ((far_d, od, zrd), (far_g, og, zrg), (far_u, ou, zru)):
        copy.wait_recv()
        mine[...] = (mine[...].astype(F32) + got[...].astype(F32)).astype(BF16)
    for copy in homeward:
        copy.wait_recv()
    for copy in locals_[len(own_w + own_r):]:
        copy.wait()
    for copy in sent:
        copy.wait_send()


def layer(cap, packed_x, packed_s, wg, wu, wd):
    half, quarter = wg.shape
    slots = 2 * cap
    width = 2 * half
    count = 2 * slots
    vmem = lambda *shape, dtype=BF16: pltpu.VMEM(shape, dtype)
    back = jax.ShapeDtypeStruct((slots, width), BF16)
    like = lambda w: jax.ShapeDtypeStruct(w.shape, BF16)
    anywhere = pl.BlockSpec(memory_space=pl.ANY)
    inside = pl.BlockSpec(memory_space=pltpu.VMEM)
    ff = 2 * quarter
    copies = 43
    return pl.pallas_call(
        functools.partial(layer_kernel, cap, half, quarter),
        out_shape=(back, back, like(wg), like(wu), like(wd)),
        in_specs=[anywhere] * 5,
        out_specs=(anywhere, anywhere, inside, inside, inside),
        scratch_shapes=[
            vmem(count, width), vmem(count, width),
            vmem(4, half, quarter), vmem(4, half, quarter), vmem(4, quarter, half),
            vmem(count, ff, dtype=F32), vmem(count, ff, dtype=F32),
            vmem(count, ff), vmem(count, 2 * ff),
        ]
        + [vmem(slots, width)] * 6
        + [vmem(2, half, quarter), vmem(2, half, quarter), vmem(2, quarter, half)] * 2
        + [vmem(half, quarter), vmem(half, quarter), vmem(quarter, half)] * 2
        + [
            pltpu.SemaphoreType.DMA((copies,)),
            pltpu.SemaphoreType.DMA((copies,)),
            pltpu.SemaphoreType.DMA((16,)),
        ],
        compiler_params=pltpu.CompilerParams(
            collective_id=0, has_side_effects=True, vmem_limit_bytes=60 * 1024 * 1024
        ),
        cost_estimate=pl.CostEstimate(
            flops=18 * count * width * ff, bytes_accessed=40 * half * quarter * 2,
            transcendentals=2 * count * ff,
        ),
    )(packed_x, packed_s, wg, wu, wd)


def layer_by_permutes(experts, capacity, packed_x, packed_s, w_gate, w_up, w_down):
    half, quarter = w_gate.shape
    slots = experts * capacity
    gate_up = jnp.concatenate([w_gate, w_up], axis=1)
    down = w_down
    gate_up_z = swap(gate_up, 4)
    down_z = swap(down, 4)

    def dispatch(packed):
        here = packed[:capacity]
        others = jnp.concatenate(
            [
                swap(packed[d * capacity : (d + 1) * capacity], 8 * d)
                for d in range(1, experts)
            ],
            axis=0,
        )
        return jnp.concatenate([here, others, swap(here, 2), swap(others, 2)], axis=0)

    rows = dispatch(packed_x)
    grads = dispatch(packed_s)

    gate_up_c, down_c = swap(gate_up, 1), swap(down, 1)
    gate_up_zc, down_zc = swap(gate_up_z, 1), swap(down_z, 1)
    w_in = jnp.concatenate(
        [
            jnp.concatenate([gate_up, gate_up_z], axis=1),
            jnp.concatenate([gate_up_c, gate_up_zc], axis=1),
        ],
        axis=0,
    )
    w_out = jnp.concatenate(
        [
            jnp.concatenate([down, down_c], axis=1),
            jnp.concatenate([down_z, down_zc], axis=1),
        ],
        axis=0,
    )

    pre = dot(rows, w_in, 1, 0)
    g = jnp.concatenate([pre[:, :quarter], pre[:, 2 * quarter : 3 * quarter]], axis=1)
    u = jnp.concatenate([pre[:, quarter : 2 * quarter], pre[:, 3 * quarter :]], axis=1)
    sg = jax.nn.sigmoid(g)
    act = (g * sg * u).astype(BF16)

    def give_back(part):
        ready = part[:slots] + swap(part[slots:].astype(BF16), 2).astype(F32)
        ready = ready.astype(BF16)
        return jnp.concatenate(
            [ready[:capacity]]
            + [
                swap(ready[d * capacity : (d + 1) * capacity], 8 * d)
                for d in range(1, experts)
            ],
            axis=0,
        )

    back_out = give_back(dot(act, w_out, 1, 0))
    d_act = dot(grads, w_out, 1, 1)
    d_gate = (d_act * u * sg * (1.0 + g * (1.0 - sg))).astype(BF16)
    d_up = (d_act * g * sg).astype(BF16)
    d_pre = jnp.concatenate(
        [d_gate[:, :quarter], d_up[:, :quarter], d_gate[:, quarter:], d_up[:, quarter:]], axis=1
    )
    back_dx = give_back(dot(d_pre, w_in, 1, 1))

    in_theirs = dot(rows[:, half:], d_pre, 0, 0).astype(BF16)
    out_theirs = dot(act, grads[:, half:], 0, 0).astype(BF16)
    in_mine = dot(rows[:, :half], d_pre, 0, 0) + swap(in_theirs, 1).astype(F32)
    out_mine = dot(act, grads[:, :half], 0, 0) + swap(out_theirs, 1).astype(F32)
    in_sum = in_mine[:, : 2 * quarter] + swap(
        in_mine[:, 2 * quarter :].astype(BF16), 4
    ).astype(F32)
    out_sum = out_mine[:quarter] + swap(out_mine[quarter:].astype(BF16), 4).astype(F32)
    grad_in = in_sum.astype(BF16)
    return back_out, back_dx, grad_in[:, :quarter], grad_in[:, quarter:], out_sum.astype(BF16)


def on_device(tokens, gates, routes, counts, w_gate, w_up, w_down, cotangent):
    peers = lax.axis_size("expert")
    tok_rows, topk = routes.shape
    width = tokens.shape[1]
    half = width // 2
    experts = peers // 8
    capacity = max(2, 3 * tok_rows * topk // (2 * experts))
    flat_n = tok_rows * topk
    slots = experts * capacity
    me = lax.axis_index("expert")
    mine, core = me // 8, me % 2

    valid = jnp.arange(tok_rows, dtype=jnp.int32) < counts[0]
    target = jnp.where(valid[:, None], routes, experts).reshape(flat_n)
    onehot = (target[:, None] == jnp.arange(experts, dtype=jnp.int32)[None, :]).astype(F32)
    earlier = (
        jnp.arange(flat_n)[:, None] > jnp.arange(flat_n)[None, :]
    ).astype(BF16)
    before = dot(earlier, onehot.astype(BF16), 1, 0)
    slot_pos = jnp.sum(before * onehot, axis=1).astype(jnp.int32)
    place = jnp.where(target < experts, (target ^ mine) * capacity + slot_pos, slots)
    put = (place[:, None] == jnp.arange(slots, dtype=jnp.int32)[None, :]).astype(BF16)
    gate_flat = gates.reshape(flat_n)
    if topk == 1:
        tok_flat, cot_flat = tokens, cotangent
    else:
        tok_flat = jnp.repeat(tokens, topk, axis=0)
        cot_flat = jnp.repeat(cotangent, topk, axis=0)
    cot_rows = cot_flat.astype(F32)
    scaled = (gate_flat[:, None] * cot_rows).astype(BF16)

    def own_first(rows):
        return jnp.where(
            core == 0, rows, jnp.concatenate([rows[:, half:], rows[:, :half]], axis=1)
        )

    packed_x = dot(put, own_first(tok_flat), 0, 0).astype(BF16)
    packed_s = dot(put, own_first(scaled), 0, 0).astype(BF16)

    if experts == 2 and capacity % 32 == 0 and half % 256 == 0 and lax.axis_size("groups") == 2:
        back_out, back_dx, grad_wg, grad_wu, grad_wd = layer(
            capacity, packed_x, packed_s, w_gate[0], w_up[0], w_down[0]
        )
    else:
        back_out, back_dx, grad_wg, grad_wu, grad_wd = layer_by_permutes(
            experts, capacity, packed_x, packed_s, w_gate[0], w_up[0], w_down[0]
        )

    out_rows = own_first(dot(put, back_out, 1, 0))
    dx_rows = own_first(dot(put, back_dx, 1, 0))
    mixed = jnp.sum(
        (gate_flat[:, None] * out_rows).reshape(tok_rows, topk, width), axis=1
    ).astype(BF16)
    grad_tokens = jnp.sum(dx_rows.reshape(tok_rows, topk, width), axis=1).astype(BF16)
    grad_gates = jnp.sum(cot_rows * out_rows, axis=1).reshape(tok_rows, topk)
    return (
        mixed,
        grad_tokens,
        grad_gates,
        grad_wg[None],
        grad_wu[None],
        grad_wd[None],
    )


def solution(mesh):
    both, rows = ("groups", "expert"), P(("groups", "expert"), None)
    block = P(both, None, None)
    weight = P("expert", None, None)
    return jax.shard_map(
        on_device,
        mesh=mesh,
        in_specs=(rows, rows, rows, P(both), weight, weight, weight, rows),
        out_specs=(rows, rows, rows, block, block, block),
        check_vma=False,
    )
```

```python
import functools

import jax
import jax.numpy as jnp
from jax import lax
from jax.experimental import pallas as pl
from jax.experimental.pallas import tpu as pltpu
from jax.sharding import PartitionSpec as P

BF16 = jnp.bfloat16
F32 = jnp.float32


def swap(value, mask):
    pairs = [(source, source ^ mask) for source in range(lax.axis_size("expert"))]
    return lax.ppermute(value, "expert", pairs)


def dot(a, b, ca, cb):
    return lax.dot_general(a, b, (((ca,), (cb,)), ((), ())), preferred_element_type=F32)


def layer_kernel(
    cap, half, quarter,
    px, ps, wg, wu, wd,
    bo, bx, og, ou, od,
    rows, grads, gates_w, ups_w, downs_w, g_buf, u_buf, act, dd,
    out_keep, out_send, out_recv, dx_keep, dx_send, dx_recv,
    tg, tu, td, rg, ru, rd, zsg, zsu, zsd, zrg, zru, zrd,
    send_sem, recv_sem, local_sem,
):
    me, group = lax.axis_index("expert"), lax.axis_index("groups")
    slots = 2 * cap
    step = cap // 2

    def partner(mask):
        return me + mask - 2 * mask * lax.rem(me // mask, 2)

    core, near, far, home = (
        {"expert": partner(1)}, {"expert": partner(2)}, {"expert": partner(4)},
        {"expert": partner(8)},
    )
    twin = {"groups": 1 - group}
    barrier = pltpu.get_barrier_semaphore()
    for other in (core, near, far, home, twin):
        pl.semaphore_signal(barrier, inc=1, device_id=other, device_id_type=pl.DeviceIdType.MESH)
    pl.semaphore_wait(barrier, 5)

    sent = []

    def send(src, dst, to):
        number = len(sent)
        copy = pltpu.make_async_remote_copy(
            src_ref=src, dst_ref=dst, send_sem=send_sem.at[number],
            recv_sem=recv_sem.at[number], device_id=to,
            device_id_type=pl.DeviceIdType.MESH,
        )
        copy.start()
        sent.append(copy)
        return copy

    locals_ = []

    def local(src, dst):
        copy = pltpu.make_async_copy(src, dst, local_sem.at[len(locals_)])
        copy.start()
        locals_.append(copy)
        return copy

    def part(ref, start, size):
        return ref.at[pl.ds(start, size)]

    over_x = [
        send(part(px, cap + i * step, step), part(rows, cap + i * step, step), home)
        for i in range(2)
    ]
    over_s = [
        send(part(ps, cap + i * step, step), part(grads, cap + i * step, step), home)
        for i in range(2)
    ]
    near_x = [send(part(px, 0, cap), part(rows, slots, cap), near)]
    near_s = [send(part(ps, 0, cap), part(grads, slots, cap), near)]
    weights = ((wg, gates_w), (wu, ups_w), (wd, downs_w))

    def group_half(ref, which):
        size = ref.shape[0] // 2
        return ref.at[pl.ds(pl.multiple_of(which * size, size), size)]

    far_w = [send(group_half(w, group), group_half(b.at[2], group), far) for w, b in weights]
    core_w = [send(w, b.at[1], core) for w, b in weights]
    own_w = [local(w, b.at[0]) for w, b in weights]
    own_r = [local(part(px, 0, cap), part(rows, 0, cap)),
             local(part(ps, 0, cap), part(grads, 0, cap))]

    for i in range(2):
        over_x[i].wait_recv()
        block = part(rows, cap + i * step, step)
        near_x.append(send(block, part(rows, slots + cap + i * step, step), near))
    twin_w = []
    for i, (w, b) in enumerate(weights):
        far_w[i].wait_recv()
        twin_w.append(send(group_half(b.at[2], group), group_half(b.at[2], group), twin))

    def forward_s(i):
        over_s[i].wait_recv()
        block = part(grads, cap + i * step, step)
        near_s.append(send(block, part(grads, slots + cap + i * step, step), near))

    def activation(q):
        columns = slice(q * quarter, (q + 1) * quarter)
        left, right = rows[:, :half], rows[:, half:]
        g = dot(left, gates_w[2 * q], 1, 0) + dot(right, gates_w[2 * q + 1], 1, 0)
        u = dot(left, ups_w[2 * q], 1, 0) + dot(right, ups_w[2 * q + 1], 1, 0)
        g_buf[:, columns] = g
        u_buf[:, columns] = u
        act[:, columns] = (g * jax.nn.sigmoid(g) * u).astype(BF16)

    forward_s(0)
    for copy in own_w + own_r:
        copy.wait()
    for copy in near_x + core_w:
        copy.wait_recv()
    activation(0)
    far_core_w = []
    for i, (w, b) in enumerate(weights):
        twin_w[i].wait_recv()
        far_core_w.append(send(b.at[2], b.at[3], core))
    forward_s(1)
    for copy in far_core_w[:2]:
        copy.wait_recv()
    activation(1)
    far_core_w[2].wait_recv()

    tile = half // 2

    def give(keep, away, arrived, make):
        for h in range(2):
            @pl.loop(0, 2)
            def _(t):
                at = pl.multiple_of(t * tile, tile)
                value = make(h, pl.ds(at, tile)).astype(BF16)
                columns = pl.ds(pl.multiple_of(h * half + t * tile, tile), tile)
                keep[:, columns] = value[:slots]
                away[:, columns] = value[slots:]
        return [
            send(part(away, at, step), part(arrived, at, step), near)
            for at in (cap, cap + step, 0, step)
        ]

    def make_out(h, columns):
        return dot(act[:, :quarter], downs_w[h, :, columns], 1, 0) + dot(
            act[:, quarter:], downs_w[2 + h, :, columns], 1, 0
        )

    near_out = give(out_keep, out_send, out_recv, make_out)

    for copy in near_s:
        copy.wait_recv()
    for q in range(2):
        columns = slice(q * quarter, (q + 1) * quarter)
        d_act = dot(grads[:, :half], downs_w[2 * q], 1, 1) + dot(
            grads[:, half:], downs_w[2 * q + 1], 1, 1
        )
        g, u = g_buf[:, columns], u_buf[:, columns]
        sg = jax.nn.sigmoid(g)
        dd[:, columns] = (d_act * u * sg * (1.0 + g * (1.0 - sg))).astype(BF16)
        dd[:, slice((2 + q) * quarter, (3 + q) * quarter)] = (d_act * g * sg).astype(BF16)

    @pl.loop(0, 2)
    def _(t):
        at = pl.multiple_of(t * tile, tile)
        value = dot(act[...], grads[:, pl.ds(pl.multiple_of(half + at, tile), tile)], 0, 0)
        value = value.astype(BF16)
        td[0, :, pl.ds(at, tile)] = value[:quarter]
        td[1, :, pl.ds(at, tile)] = value[quarter:]

    core_d = [send(td.at[q], rd.at[q], core) for q in (1, 0)]
    width_step = 256

    @pl.loop(0, half // width_step)
    def _(t):
        at = pl.multiple_of(t * width_step, width_step)
        value = dot(rows[:, pl.ds(pl.multiple_of(half + at, width_step), width_step)], dd[...], 0, 0)
        value = value.astype(BF16)
        for q in range(2):
            tg[q, pl.ds(at, width_step)] = value[:, q * quarter : (q + 1) * quarter]
            tu[q, pl.ds(at, width_step)] = value[:, (2 + q) * quarter : (3 + q) * quarter]

    core_g = [send(tg.at[q], rg.at[q], core) for q in (1, 0)]
    core_u = [send(tu.at[q], ru.at[q], core) for q in (1, 0)]

    homeward = []
    places = (cap, cap + step, 0, step)

    def finish(keep, arrived, copies, result, which):
        for i in which:
            at = places[i]
            copies[i].wait_recv()
            total = keep[at : at + step].astype(F32) + arrived[at : at + step].astype(F32)
            keep[at : at + step] = total.astype(BF16)
            if at >= cap:
                homeward.append(send(part(keep, at, step), part(result, at, step), home))
            else:
                local(part(keep, at, step), part(result, at, step))

    finish(out_keep, out_recv, near_out, bo, (0, 1))

    for copy in core_d:
        copy.wait_recv()

    @pl.loop(0, 2)
    def _(t):
        at = pl.multiple_of(t * tile, tile)
        value = dot(act[...], grads[:, pl.ds(at, tile)], 0, 0)
        od[:, pl.ds(at, tile)] = (value[:quarter] + rd[0, :, pl.ds(at, tile)].astype(F32)).astype(BF16)
        zsd[:, pl.ds(at, tile)] = (value[quarter:] + rd[1, :, pl.ds(at, tile)].astype(F32)).astype(BF16)

    far_d = send(zsd, zrd, far)

    def make_dx(h, columns):
        value = dot(dd[:, :quarter], gates_w[h, columns], 1, 1)
        value = value + dot(dd[:, quarter : 2 * quarter], gates_w[2 + h, columns], 1, 1)
        value = value + dot(dd[:, 2 * quarter : 3 * quarter], ups_w[h, columns], 1, 1)
        return value + dot(dd[:, 3 * quarter :], ups_w[2 + h, columns], 1, 1)

    near_dx = give(dx_keep, dx_send, dx_recv, make_dx)

    for copy in core_g + core_u:
        copy.wait_recv()

    @pl.loop(0, half // width_step)
    def _(t):
        at = pl.ds(pl.multiple_of(t * width_step, width_step), width_step)
        value = dot(rows[:, at], dd[...], 0, 0)
        for column, got, mine, away in ((0, rg, og, zsg), (2, ru, ou, zsu)):
            first = value[:, column * quarter : (column + 1) * quarter]
            second = value[:, (column + 1) * quarter : (column + 2) * quarter]
            mine[at] = (first + got[0, at].astype(F32)).astype(BF16)
            away[at] = (second + got[1, at].astype(F32)).astype(BF16)

    far_g = send(zsg, zrg, far)
    far_u = send(zsu, zru, far)

    finish(dx_keep, dx_recv, near_dx, bx, (0, 1))
    finish(out_keep, out_recv, near_out, bo, (2, 3))
    finish(dx_keep, dx_recv, near_dx, bx, (2, 3))

    for copy, mine, got in ((far_d, od, zrd), (far_g, og, zrg), (far_u, ou, zru)):
        copy.wait_recv()
        mine[...] = (mine[...].astype(F32) + got[...].astype(F32)).astype(BF16)
    for copy in homeward:
        copy.wait_recv()
    for copy in locals_[len(own_w + own_r):]:
        copy.wait()
    for copy in sent:
        copy.wait_send()


def layer(cap, packed_x, packed_s, wg, wu, wd):
    half, quarter = wg.shape
    slots = 2 * cap
    width = 2 * half
    count = 2 * slots
    vmem = lambda *shape, dtype=BF16: pltpu.VMEM(shape, dtype)
    back = jax.ShapeDtypeStruct((slots, width), BF16)
    like = lambda w: jax.ShapeDtypeStruct(w.shape, BF16)
    anywhere = pl.BlockSpec(memory_space=pl.ANY)
    inside = pl.BlockSpec(memory_space=pltpu.VMEM)
    ff = 2 * quarter
    copies = 43
    return pl.pallas_call(
        functools.partial(layer_kernel, cap, half, quarter),
        out_shape=(back, back, like(wg), like(wu), like(wd)),
        in_specs=[anywhere] * 5,
        out_specs=(anywhere, anywhere, inside, inside, inside),
        scratch_shapes=[
            vmem(count, width), vmem(count, width),
            vmem(4, half, quarter), vmem(4, half, quarter), vmem(4, quarter, half),
            vmem(count, ff, dtype=F32), vmem(count, ff, dtype=F32),
            vmem(count, ff), vmem(count, 2 * ff),
        ]
        + [vmem(slots, width)] * 6
        + [vmem(2, half, quarter), vmem(2, half, quarter), vmem(2, quarter, half)] * 2
        + [vmem(half, quarter), vmem(half, quarter), vmem(quarter, half)] * 2
        + [
            pltpu.SemaphoreType.DMA((copies,)),
            pltpu.SemaphoreType.DMA((copies,)),
            pltpu.SemaphoreType.DMA((16,)),
        ],
        compiler_params=pltpu.CompilerParams(
            collective_id=0, has_side_effects=True, vmem_limit_bytes=60 * 1024 * 1024
        ),
        cost_estimate=pl.CostEstimate(
            flops=18 * count * width * ff, bytes_accessed=40 * half * quarter * 2,
            transcendentals=2 * count * ff,
        ),
    )(packed_x, packed_s, wg, wu, wd)


def layer_by_permutes(experts, capacity, packed_x, packed_s, w_gate, w_up, w_down):
    half, quarter = w_gate.shape
    slots = experts * capacity
    gate_up = jnp.concatenate([w_gate, w_up], axis=1)
    down = w_down
    gate_up_z = swap(gate_up, 4)
    down_z = swap(down, 4)

    def dispatch(packed):
        here = packed[:capacity]
        others = jnp.concatenate(
            [
                swap(packed[d * capacity : (d + 1) * capacity], 8 * d)
                for d in range(1, experts)
            ],
            axis=0,
        )
        return jnp.concatenate([here, others, swap(here, 2), swap(others, 2)], axis=0)

    rows = dispatch(packed_x)
    grads = dispatch(packed_s)

    gate_up_c, down_c = swap(gate_up, 1), swap(down, 1)
    gate_up_zc, down_zc = swap(gate_up_z, 1), swap(down_z, 1)
    w_in = jnp.concatenate(
        [
            jnp.concatenate([gate_up, gate_up_z], axis=1),
            jnp.concatenate([gate_up_c, gate_up_zc], axis=1),
        ],
        axis=0,
    )
    w_out = jnp.concatenate(
        [
            jnp.concatenate([down, down_c], axis=1),
            jnp.concatenate([down_z, down_zc], axis=1),
        ],
        axis=0,
    )

    pre = dot(rows, w_in, 1, 0)
    g = jnp.concatenate([pre[:, :quarter], pre[:, 2 * quarter : 3 * quarter]], axis=1)
    u = jnp.concatenate([pre[:, quarter : 2 * quarter], pre[:, 3 * quarter :]], axis=1)
    sg = jax.nn.sigmoid(g)
    act = (g * sg * u).astype(BF16)

    def give_back(part):
        ready = part[:slots] + swap(part[slots:].astype(BF16), 2).astype(F32)
        ready = ready.astype(BF16)
        return jnp.concatenate(
            [ready[:capacity]]
            + [
                swap(ready[d * capacity : (d + 1) * capacity], 8 * d)
                for d in range(1, experts)
            ],
            axis=0,
        )

    back_out = give_back(dot(act, w_out, 1, 0))
    d_act = dot(grads, w_out, 1, 1)
    d_gate = (d_act * u * sg * (1.0 + g * (1.0 - sg))).astype(BF16)
    d_up = (d_act * g * sg).astype(BF16)
    d_pre = jnp.concatenate(
        [d_gate[:, :quarter], d_up[:, :quarter], d_gate[:, quarter:], d_up[:, quarter:]], axis=1
    )
    back_dx = give_back(dot(d_pre, w_in, 1, 1))

    in_theirs = dot(rows[:, half:], d_pre, 0, 0).astype(BF16)
    out_theirs = dot(act, grads[:, half:], 0, 0).astype(BF16)
    in_mine = dot(rows[:, :half], d_pre, 0, 0) + swap(in_theirs, 1).astype(F32)
    out_mine = dot(act, grads[:, :half], 0, 0) + swap(out_theirs, 1).astype(F32)
    in_sum = in_mine[:, : 2 * quarter] + swap(
        in_mine[:, 2 * quarter :].astype(BF16), 4
    ).astype(F32)
    out_sum = out_mine[:quarter] + swap(out_mine[quarter:].astype(BF16), 4).astype(F32)
    grad_in = in_sum.astype(BF16)
    return back_out, back_dx, grad_in[:, :quarter], grad_in[:, quarter:], out_sum.astype(BF16)


def on_device(tokens, gates, routes, counts, w_gate, w_up, w_down, cotangent):
    peers = lax.axis_size("expert")
    tok_rows, topk = routes.shape
    width = tokens.shape[1]
    half = width // 2
    experts = peers // 8
    capacity = max(2, 3 * tok_rows * topk // (2 * experts))
    flat_n = tok_rows * topk
    slots = experts * capacity
    me = lax.axis_index("expert")
    mine, core = me // 8, me % 2

    valid = jnp.arange(tok_rows, dtype=jnp.int32) < counts[0]
    target = jnp.where(valid[:, None], routes, experts).reshape(flat_n)
    onehot = (target[:, None] == jnp.arange(experts, dtype=jnp.int32)[None, :]).astype(F32)
    earlier = (
        jnp.arange(flat_n)[:, None] > jnp.arange(flat_n)[None, :]
    ).astype(BF16)
    before = dot(earlier, onehot.astype(BF16), 1, 0)
    slot_pos = jnp.sum(before * onehot, axis=1).astype(jnp.int32)
    place = jnp.where(target < experts, (target ^ mine) * capacity + slot_pos, slots)
    put = (place[:, None] == jnp.arange(slots, dtype=jnp.int32)[None, :]).astype(BF16)
    gate_flat = gates.reshape(flat_n)
    if topk == 1:
        tok_flat, cot_flat = tokens, cotangent
    else:
        tok_flat = jnp.repeat(tokens, topk, axis=0)
        cot_flat = jnp.repeat(cotangent, topk, axis=0)
    cot_rows = cot_flat.astype(F32)
    scaled = (gate_flat[:, None] * cot_rows).astype(BF16)

    def own_first(rows):
        return jnp.where(
            core == 0, rows, jnp.concatenate([rows[:, half:], rows[:, :half]], axis=1)
        )

    packed_x = dot(put, own_first(tok_flat), 0, 0).astype(BF16)
    packed_s = dot(put, own_first(scaled), 0, 0).astype(BF16)

    if experts == 2 and capacity % 32 == 0 and half % 256 == 0 and lax.axis_size("groups") == 2:
        back_out, back_dx, grad_wg, grad_wu, grad_wd = layer(
            capacity, packed_x, packed_s, w_gate[0], w_up[0], w_down[0]
        )
    else:
        back_out, back_dx, grad_wg, grad_wu, grad_wd = layer_by_permutes(
            experts, capacity, packed_x, packed_s, w_gate[0], w_up[0], w_down[0]
        )

    out_rows = own_first(dot(put, back_out, 1, 0))
    dx_rows = own_first(dot(put, back_dx, 1, 0))
    mixed = jnp.sum(
        (gate_flat[:, None] * out_rows).reshape(tok_rows, topk, width), axis=1
    ).astype(BF16)
    grad_tokens = jnp.sum(dx_rows.reshape(tok_rows, topk, width), axis=1).astype(BF16)
    grad_gates = jnp.sum(cot_rows * out_rows, axis=1).reshape(tok_rows, topk)
    return (
        mixed,
        grad_tokens,
        grad_gates,
        grad_wg[None],
        grad_wu[None],
        grad_wd[None],
    )


def solution(mesh):
    both, rows = ("groups", "expert"), P(("groups", "expert"), None)
    block = P(both, None, None)
    weight = P("expert", None, None)
    return jax.shard_map(
        on_device,
        mesh=mesh,
        in_specs=(rows, rows, rows, P(both), weight, weight, weight, rows),
        out_specs=(rows, rows, rows, block, block, block),
        check_vma=False,
    )
```

```python
import functools

import jax
import jax.numpy as jnp
from jax import lax
from jax.experimental import pallas as pl
from jax.experimental.pallas import tpu as pltpu
from jax.sharding import PartitionSpec as P

BF16 = jnp.bfloat16
F32 = jnp.float32


def swap(value, mask):
    pairs = [(source, source ^ mask) for source in range(lax.axis_size("expert"))]
    return lax.ppermute(value, "expert", pairs)


def dot(a, b, ca, cb):
    return lax.dot_general(a, b, (((ca,), (cb,)), ((), ())), preferred_element_type=F32)


def layer_kernel(
    cap, half, quarter,
    px, ps, wg, wu, wd,
    bo, bx, og, ou, od, zrg, zru, zrd,
    rows, grads, gates_w, ups_w, downs_w, g_buf, u_buf, act, dd,
    out_keep, out_send, out_recv, dx_keep, dx_send, dx_recv,
    tg, tu, td, rg, ru, rd, zsg, zsu, zsd,
    send_sem, recv_sem, local_sem,
):
    me, group = lax.axis_index("expert"), lax.axis_index("groups")
    slots = 2 * cap
    step = cap // 2

    def partner(mask):
        return me + mask - 2 * mask * lax.rem(me // mask, 2)

    core, near, far, home = (
        {"expert": partner(1)}, {"expert": partner(2)}, {"expert": partner(4)},
        {"expert": partner(8)},
    )
    twin = {"groups": 1 - group}
    barrier = pltpu.get_barrier_semaphore()
    for other in (core, near, far, home, twin):
        pl.semaphore_signal(barrier, inc=1, device_id=other, device_id_type=pl.DeviceIdType.MESH)
    pl.semaphore_wait(barrier, 5)

    sent = []

    def send(src, dst, to):
        number = len(sent)
        copy = pltpu.make_async_remote_copy(
            src_ref=src, dst_ref=dst, send_sem=send_sem.at[number],
            recv_sem=recv_sem.at[number], device_id=to,
            device_id_type=pl.DeviceIdType.MESH,
        )
        copy.start()
        sent.append(copy)
        return copy

    locals_ = []

    def local(src, dst):
        copy = pltpu.make_async_copy(src, dst, local_sem.at[len(locals_)])
        copy.start()
        locals_.append(copy)
        return copy

    def part(ref, start, size):
        return ref.at[pl.ds(start, size)]

    over_x = [
        send(part(px, cap + i * step, step), part(rows, cap + i * step, step), home)
        for i in range(2)
    ]
    near_x = [send(part(px, 0, cap), part(rows, slots, cap), near)]
    near_s = [send(part(ps, 0, cap), part(grads, slots, cap), near)]
    weights = ((wg, gates_w), (wu, ups_w), (wd, downs_w))

    def group_half(ref, which):
        size = ref.shape[0] // 2
        return ref.at[pl.ds(pl.multiple_of(which * size, size), size)]

    far_w = [
        send(group_half(w, group), group_half(b.at[2], group), far) for w, b in weights[:2]
    ]
    core_w = [send(w, b.at[1], core) for w, b in weights]
    own_w = [local(w, b.at[0]) for w, b in weights]
    own_r = [local(part(px, 0, cap), part(rows, 0, cap)),
             local(part(ps, 0, cap), part(grads, 0, cap))]

    over_s = []
    for i in range(2):
        over_x[i].wait_recv()
        over_s.append(
            send(part(ps, cap + i * step, step), part(grads, cap + i * step, step), home)
        )
        block = part(rows, cap + i * step, step)
        near_x.append(send(block, part(rows, slots + cap + i * step, step), near))
    twin_w = []
    for i, (w, b) in enumerate(weights):
        far_w[i].wait_recv()
        if i == 0:
            far_w.append(send(group_half(wd, group), group_half(downs_w.at[2], group), far))
        twin_w.append(send(group_half(b.at[2], group), group_half(b.at[2], group), twin))

    def forward_s(i):
        over_s[i].wait_recv()
        block = part(grads, cap + i * step, step)
        near_s.append(send(block, part(grads, slots + cap + i * step, step), near))

    def activation(q):
        columns = slice(q * quarter, (q + 1) * quarter)
        left, right = rows[:, :half], rows[:, half:]
        g = dot(left, gates_w[2 * q], 1, 0) + dot(right, gates_w[2 * q + 1], 1, 0)
        u = dot(left, ups_w[2 * q], 1, 0) + dot(right, ups_w[2 * q + 1], 1, 0)
        g_buf[:, columns] = g
        u_buf[:, columns] = u
        act[:, columns] = (g * jax.nn.sigmoid(g) * u).astype(BF16)

    forward_s(0)
    for copy in own_w + own_r:
        copy.wait()
    for copy in near_x + core_w:
        copy.wait_recv()
    activation(0)
    far_core_w = []
    for i, (w, b) in enumerate(weights):
        twin_w[i].wait_recv()
        far_core_w.append(send(b.at[2], b.at[3], core))
    forward_s(1)
    for copy in far_core_w[:2]:
        copy.wait_recv()
    activation(1)
    far_core_w[2].wait_recv()

    tile = half // 2

    def give(keep, away, arrived, make):
        for h in range(2):
            @pl.loop(0, 2)
            def _(t):
                at = pl.multiple_of(t * tile, tile)
                value = make(h, pl.ds(at, tile)).astype(BF16)
                columns = pl.ds(pl.multiple_of(h * half + t * tile, tile), tile)
                keep[:, columns] = value[:slots]
                away[:, columns] = value[slots:]
        return [
            send(part(away, at, step), part(arrived, at, step), near)
            for at in (cap, cap + step)
        ]

    def make_out(h, columns):
        return dot(act[:, :quarter], downs_w[h, :, columns], 1, 0) + dot(
            act[:, quarter:], downs_w[2 + h, :, columns], 1, 0
        )

    near_out = give(out_keep, out_send, out_recv, make_out)

    for copy in near_s:
        copy.wait_recv()
    for q in range(2):
        columns = slice(q * quarter, (q + 1) * quarter)
        d_act = dot(grads[:, :half], downs_w[2 * q], 1, 1) + dot(
            grads[:, half:], downs_w[2 * q + 1], 1, 1
        )
        g, u = g_buf[:, columns], u_buf[:, columns]
        sg = jax.nn.sigmoid(g)
        dd[:, columns] = (d_act * u * sg * (1.0 + g * (1.0 - sg))).astype(BF16)
        dd[:, slice((2 + q) * quarter, (3 + q) * quarter)] = (d_act * g * sg).astype(BF16)

    @pl.loop(0, 2)
    def _(t):
        at = pl.multiple_of(t * tile, tile)
        value = dot(act[...], grads[:, pl.ds(pl.multiple_of(half + at, tile), tile)], 0, 0)
        value = value.astype(BF16)
        td[0, :, pl.ds(at, tile)] = value[:quarter]
        td[1, :, pl.ds(at, tile)] = value[quarter:]

    core_d = [send(td.at[q], rd.at[q], core) for q in (1, 0)]
    width_step = 256

    @pl.loop(0, half // width_step)
    def _(t):
        at = pl.multiple_of(t * width_step, width_step)
        value = dot(rows[:, pl.ds(pl.multiple_of(half + at, width_step), width_step)], dd[...], 0, 0)
        value = value.astype(BF16)
        for q in range(2):
            tg[q, pl.ds(at, width_step)] = value[:, q * quarter : (q + 1) * quarter]
            tu[q, pl.ds(at, width_step)] = value[:, (2 + q) * quarter : (3 + q) * quarter]

    core_g = [send(tg.at[q], rg.at[q], core) for q in (1, 0)]
    core_u = [send(tu.at[q], ru.at[q], core) for q in (1, 0)]

    homeward = []
    places = (cap, cap + step, 0, step)

    def finish(keep, away, arrived, copies, result, which):
        for i in which:
            at = places[i]
            copies[i].wait_recv()
            total = keep[at : at + step].astype(F32) + arrived[at : at + step].astype(F32)
            keep[at : at + step] = total.astype(BF16)
            if at >= cap:
                later = places[i + 2]
                homeward.append(send(part(keep, at, step), part(result, at, step), home))
                copies.append(send(part(away, later, step), part(arrived, later, step), near))
            else:
                local(part(keep, at, step), part(result, at, step))

    finish(out_keep, out_send, out_recv, near_out, bo, (0, 1))

    for copy in core_d:
        copy.wait_recv()

    @pl.loop(0, 2)
    def _(t):
        at = pl.multiple_of(t * tile, tile)
        value = dot(act[...], grads[:, pl.ds(at, tile)], 0, 0)
        od[:, pl.ds(at, tile)] = (value[:quarter] + rd[0, :, pl.ds(at, tile)].astype(F32)).astype(BF16)
        zsd[:, pl.ds(at, tile)] = (value[quarter:] + rd[1, :, pl.ds(at, tile)].astype(F32)).astype(BF16)

    far_d = send(zsd, zrd, far)

    def make_dx(h, columns):
        value = dot(dd[:, :quarter], gates_w[h, columns], 1, 1)
        value = value + dot(dd[:, quarter : 2 * quarter], gates_w[2 + h, columns], 1, 1)
        value = value + dot(dd[:, 2 * quarter : 3 * quarter], ups_w[h, columns], 1, 1)
        return value + dot(dd[:, 3 * quarter :], ups_w[2 + h, columns], 1, 1)

    near_dx = give(dx_keep, dx_send, dx_recv, make_dx)

    for copy in core_g + core_u:
        copy.wait_recv()

    @pl.loop(0, half // width_step)
    def _(t):
        at = pl.ds(pl.multiple_of(t * width_step, width_step), width_step)
        value = dot(rows[:, at], dd[...], 0, 0)
        for column, got, mine, away in ((0, rg, og, zsg), (2, ru, ou, zsu)):
            first = value[:, column * quarter : (column + 1) * quarter]
            second = value[:, (column + 1) * quarter : (column + 2) * quarter]
            mine[at] = (first + got[0, at].astype(F32)).astype(BF16)
            away[at] = (second + got[1, at].astype(F32)).astype(BF16)

    far_g = send(zsg, zrg, far)
    far_u = send(zsu, zru, far)

    finish(dx_keep, dx_send, dx_recv, near_dx, bx, (0, 1))
    finish(out_keep, out_send, out_recv, near_out, bo, (2, 3))
    finish(dx_keep, dx_send, dx_recv, near_dx, bx, (2, 3))

    for copy in (far_d, far_g, far_u):
        copy.wait_recv()
    for copy in homeward:
        copy.wait_recv()
    for copy in locals_[len(own_w + own_r):]:
        copy.wait()
    for copy in sent:
        copy.wait_send()


def layer(cap, packed_x, packed_s, wg, wu, wd):
    half, quarter = wg.shape
    slots = 2 * cap
    width = 2 * half
    count = 2 * slots
    vmem = lambda *shape, dtype=BF16: pltpu.VMEM(shape, dtype)
    back = jax.ShapeDtypeStruct((slots, width), BF16)
    like = lambda w: jax.ShapeDtypeStruct(w.shape, BF16)
    anywhere = pl.BlockSpec(memory_space=pl.ANY)
    inside = pl.BlockSpec(memory_space=pltpu.VMEM)
    ff = 2 * quarter
    copies = 43
    back_out, back_dx, *sums = pl.pallas_call(
        functools.partial(layer_kernel, cap, half, quarter),
        out_shape=(back, back) + (like(wg), like(wu), like(wd)) * 2,
        in_specs=[anywhere] * 5,
        out_specs=(anywhere,) * 2 + (inside,) * 3 + (anywhere,) * 3,
        scratch_shapes=[
            vmem(count, width), vmem(count, width),
            vmem(4, half, quarter), vmem(4, half, quarter), vmem(4, quarter, half),
            vmem(count, ff, dtype=F32), vmem(count, ff, dtype=F32),
            vmem(count, ff), vmem(count, 2 * ff),
        ]
        + [vmem(slots, width)] * 6
        + [vmem(2, half, quarter), vmem(2, half, quarter), vmem(2, quarter, half)] * 2
        + [vmem(half, quarter), vmem(half, quarter), vmem(quarter, half)]
        + [
            pltpu.SemaphoreType.DMA((copies,)),
            pltpu.SemaphoreType.DMA((copies,)),
            pltpu.SemaphoreType.DMA((16,)),
        ],
        compiler_params=pltpu.CompilerParams(
            collective_id=0, has_side_effects=True, vmem_limit_bytes=60 * 1024 * 1024
        ),
        cost_estimate=pl.CostEstimate(
            flops=18 * count * width * ff, bytes_accessed=40 * half * quarter * 2,
            transcendentals=2 * count * ff,
        ),
    )(packed_x, packed_s, wg, wu, wd)
    added = [(a.astype(F32) + b.astype(F32)).astype(BF16) for a, b in zip(sums[:3], sums[3:])]
    return back_out, back_dx, *added


def layer_by_permutes(experts, capacity, packed_x, packed_s, w_gate, w_up, w_down):
    half, quarter = w_gate.shape
    slots = experts * capacity
    gate_up = jnp.concatenate([w_gate, w_up], axis=1)
    down = w_down
    gate_up_z = swap(gate_up, 4)
    down_z = swap(down, 4)

    def dispatch(packed):
        here = packed[:capacity]
        others = jnp.concatenate(
            [
                swap(packed[d * capacity : (d + 1) * capacity], 8 * d)
                for d in range(1, experts)
            ],
            axis=0,
        )
        return jnp.concatenate([here, others, swap(here, 2), swap(others, 2)], axis=0)

    rows = dispatch(packed_x)
    grads = dispatch(packed_s)

    gate_up_c, down_c = swap(gate_up, 1), swap(down, 1)
    gate_up_zc, down_zc = swap(gate_up_z, 1), swap(down_z, 1)
    w_in = jnp.concatenate(
        [
            jnp.concatenate([gate_up, gate_up_z], axis=1),
            jnp.concatenate([gate_up_c, gate_up_zc], axis=1),
        ],
        axis=0,
    )
    w_out = jnp.concatenate(
        [
            jnp.concatenate([down, down_c], axis=1),
            jnp.concatenate([down_z, down_zc], axis=1),
        ],
        axis=0,
    )

    pre = dot(rows, w_in, 1, 0)
    g = jnp.concatenate([pre[:, :quarter], pre[:, 2 * quarter : 3 * quarter]], axis=1)
    u = jnp.concatenate([pre[:, quarter : 2 * quarter], pre[:, 3 * quarter :]], axis=1)
    sg = jax.nn.sigmoid(g)
    act = (g * sg * u).astype(BF16)

    def give_back(part):
        ready = part[:slots] + swap(part[slots:].astype(BF16), 2).astype(F32)
        ready = ready.astype(BF16)
        return jnp.concatenate(
            [ready[:capacity]]
            + [
                swap(ready[d * capacity : (d + 1) * capacity], 8 * d)
                for d in range(1, experts)
            ],
            axis=0,
        )

    back_out = give_back(dot(act, w_out, 1, 0))
    d_act = dot(grads, w_out, 1, 1)
    d_gate = (d_act * u * sg * (1.0 + g * (1.0 - sg))).astype(BF16)
    d_up = (d_act * g * sg).astype(BF16)
    d_pre = jnp.concatenate(
        [d_gate[:, :quarter], d_up[:, :quarter], d_gate[:, quarter:], d_up[:, quarter:]], axis=1
    )
    back_dx = give_back(dot(d_pre, w_in, 1, 1))

    in_theirs = dot(rows[:, half:], d_pre, 0, 0).astype(BF16)
    out_theirs = dot(act, grads[:, half:], 0, 0).astype(BF16)
    in_mine = dot(rows[:, :half], d_pre, 0, 0) + swap(in_theirs, 1).astype(F32)
    out_mine = dot(act, grads[:, :half], 0, 0) + swap(out_theirs, 1).astype(F32)
    in_sum = in_mine[:, : 2 * quarter] + swap(
        in_mine[:, 2 * quarter :].astype(BF16), 4
    ).astype(F32)
    out_sum = out_mine[:quarter] + swap(out_mine[quarter:].astype(BF16), 4).astype(F32)
    grad_in = in_sum.astype(BF16)
    return back_out, back_dx, grad_in[:, :quarter], grad_in[:, quarter:], out_sum.astype(BF16)


def on_device(tokens, gates, routes, counts, w_gate, w_up, w_down, cotangent):
    peers = lax.axis_size("expert")
    tok_rows, topk = routes.shape
    width = tokens.shape[1]
    half = width // 2
    experts = peers // 8
    capacity = max(2, 3 * tok_rows * topk // (2 * experts))
    flat_n = tok_rows * topk
    slots = experts * capacity
    me = lax.axis_index("expert")
    mine, core = me // 8, me % 2

    valid = jnp.arange(tok_rows, dtype=jnp.int32) < counts[0]
    target = jnp.where(valid[:, None], routes, experts).reshape(flat_n)
    onehot = (target[:, None] == jnp.arange(experts, dtype=jnp.int32)[None, :]).astype(F32)
    earlier = (
        jnp.arange(flat_n)[:, None] > jnp.arange(flat_n)[None, :]
    ).astype(BF16)
    before = dot(earlier, onehot.astype(BF16), 1, 0)
    slot_pos = jnp.sum(before * onehot, axis=1).astype(jnp.int32)
    place = jnp.where(target < experts, (target ^ mine) * capacity + slot_pos, slots)
    put = (place[:, None] == jnp.arange(slots, dtype=jnp.int32)[None, :]).astype(BF16)
    gate_flat = gates.reshape(flat_n)
    if topk == 1:
        tok_flat, cot_flat = tokens, cotangent
    else:
        tok_flat = jnp.repeat(tokens, topk, axis=0)
        cot_flat = jnp.repeat(cotangent, topk, axis=0)
    cot_rows = cot_flat.astype(F32)
    scaled = (gate_flat[:, None] * cot_rows).astype(BF16)

    def own_first(rows):
        return jnp.where(
            core == 0, rows, jnp.concatenate([rows[:, half:], rows[:, :half]], axis=1)
        )

    packed_x = dot(put, own_first(tok_flat), 0, 0).astype(BF16)
    packed_s = dot(put, own_first(scaled), 0, 0).astype(BF16)

    if experts == 2 and capacity % 32 == 0 and half % 256 == 0 and lax.axis_size("groups") == 2:
        back_out, back_dx, grad_wg, grad_wu, grad_wd = layer(
            capacity, packed_x, packed_s, w_gate[0], w_up[0], w_down[0]
        )
    else:
        back_out, back_dx, grad_wg, grad_wu, grad_wd = layer_by_permutes(
            experts, capacity, packed_x, packed_s, w_gate[0], w_up[0], w_down[0]
        )

    out_rows = own_first(dot(put, back_out, 1, 0))
    dx_rows = own_first(dot(put, back_dx, 1, 0))
    mixed = jnp.sum(
        (gate_flat[:, None] * out_rows).reshape(tok_rows, topk, width), axis=1
    ).astype(BF16)
    grad_tokens = jnp.sum(dx_rows.reshape(tok_rows, topk, width), axis=1).astype(BF16)
    grad_gates = jnp.sum(cot_rows * out_rows, axis=1).reshape(tok_rows, topk)
    return (
        mixed,
        grad_tokens,
        grad_gates,
        grad_wg[None],
        grad_wu[None],
        grad_wd[None],
    )


def solution(mesh):
    both, rows = ("groups", "expert"), P(("groups", "expert"), None)
    block = P(both, None, None)
    weight = P("expert", None, None)
    return jax.shard_map(
        on_device,
        mesh=mesh,
        in_specs=(rows, rows, rows, P(both), weight, weight, weight, rows),
        out_specs=(rows, rows, rows, block, block, block),
        check_vma=False,
    )
```

```python
import functools

import jax
import jax.numpy as jnp
from jax import lax
from jax.experimental import pallas as pl
from jax.experimental.pallas import tpu as pltpu
from jax.sharding import PartitionSpec as P

BF16 = jnp.bfloat16
F32 = jnp.float32


def swap(value, mask):
    pairs = [(source, source ^ mask) for source in range(lax.axis_size("expert"))]
    return lax.ppermute(value, "expert", pairs)


def dot(a, b, ca, cb):
    return lax.dot_general(a, b, (((ca,), (cb,)), ((), ())), preferred_element_type=F32)


def layer_kernel(
    cap, half, quarter,
    px, ps, wg, wu, wd,
    bo, bx, og, ou, od,
    rows, grads, gates_w, ups_w, downs_w, g_buf, u_buf, act, dd,
    out_keep, out_send, out_recv, dx_keep, dx_send, dx_recv,
    tg, tu, td, rg, ru, rd, zsg, zsu, zsd, zrg, zru, zrd,
    send_sem, recv_sem, local_sem,
):
    me, group = lax.axis_index("expert"), lax.axis_index("groups")
    slots = 2 * cap
    step = cap // 2

    def partner(mask):
        return me + mask - 2 * mask * lax.rem(me // mask, 2)

    core, near, far, home = (
        {"expert": partner(1)}, {"expert": partner(2)}, {"expert": partner(4)},
        {"expert": partner(8)},
    )
    twin = {"groups": 1 - group}
    barrier = pltpu.get_barrier_semaphore()
    for other in (core, near, far, home, twin):
        pl.semaphore_signal(barrier, inc=1, device_id=other, device_id_type=pl.DeviceIdType.MESH)
    pl.semaphore_wait(barrier, 5)

    sent = []

    def send(src, dst, to):
        number = len(sent)
        copy = pltpu.make_async_remote_copy(
            src_ref=src, dst_ref=dst, send_sem=send_sem.at[number],
            recv_sem=recv_sem.at[number], device_id=to,
            device_id_type=pl.DeviceIdType.MESH,
        )
        copy.start()
        sent.append(copy)
        return copy

    locals_ = []

    def local(src, dst):
        copy = pltpu.make_async_copy(src, dst, local_sem.at[len(locals_)])
        copy.start()
        locals_.append(copy)
        return copy

    def part(ref, start, size):
        return ref.at[pl.ds(start, size)]

    over_x = [
        send(part(px, cap + i * step, step), part(rows, cap + i * step, step), home)
        for i in range(2)
    ]
    near_x = [send(part(px, 0, cap), part(rows, slots, cap), near)]
    near_s = [send(part(ps, 0, cap), part(grads, slots, cap), near)]
    weights = ((wg, gates_w), (wu, ups_w), (wd, downs_w))

    def group_half(ref, which):
        size = ref.shape[0] // 2
        return ref.at[pl.ds(pl.multiple_of(which * size, size), size)]

    far_w = [send(group_half(w, group), group_half(b.at[2], group), far) for w, b in weights]
    core_w = [send(w, b.at[1], core) for w, b in weights]
    own_w = [local(w, b.at[0]) for w, b in weights]
    own_r = [local(part(px, 0, cap), part(rows, 0, cap)),
             local(part(ps, 0, cap), part(grads, 0, cap))]

    over_s = []
    for i in range(2):
        over_x[i].wait_recv()
        over_s.append(
            send(part(ps, cap + i * step, step), part(grads, cap + i * step, step), home)
        )
        block = part(rows, cap + i * step, step)
        near_x.append(send(block, part(rows, slots + cap + i * step, step), near))
    twin_w = []
    for i, (w, b) in enumerate(weights):
        far_w[i].wait_recv()
        twin_w.append(send(group_half(b.at[2], group), group_half(b.at[2], group), twin))

    def forward_s(i):
        over_s[i].wait_recv()
        block = part(grads, cap + i * step, step)
        near_s.append(send(block, part(grads, slots + cap + i * step, step), near))

    def activation(q):
        columns = slice(q * quarter, (q + 1) * quarter)
        left, right = rows[:, :half], rows[:, half:]
        g = dot(left, gates_w[2 * q], 1, 0) + dot(right, gates_w[2 * q + 1], 1, 0)
        u = dot(left, ups_w[2 * q], 1, 0) + dot(right, ups_w[2 * q + 1], 1, 0)
        g_buf[:, columns] = g
        u_buf[:, columns] = u
        act[:, columns] = (g * jax.nn.sigmoid(g) * u).astype(BF16)

    forward_s(0)
    for copy in own_w + own_r:
        copy.wait()
    for copy in near_x + core_w:
        copy.wait_recv()
    activation(0)
    far_core_w = []
    for i, (w, b) in enumerate(weights):
        twin_w[i].wait_recv()
        far_core_w.append(send(b.at[2], b.at[3], core))
    forward_s(1)
    for copy in far_core_w[:2]:
        copy.wait_recv()
    activation(1)
    far_core_w[2].wait_recv()

    tile = half // 2

    def give(keep, away, arrived, make):
        for h in range(2):
            @pl.loop(0, 2)
            def _(t):
                at = pl.multiple_of(t * tile, tile)
                value = make(h, pl.ds(at, tile)).astype(BF16)
                columns = pl.ds(pl.multiple_of(h * half + t * tile, tile), tile)
                keep[:, columns] = value[:slots]
                away[:, columns] = value[slots:]
        return [
            send(part(away, at, step), part(arrived, at, step), near)
            for at in (cap, cap + step, 0, step)
        ]

    def make_out(h, columns):
        return dot(act[:, :quarter], downs_w[h, :, columns], 1, 0) + dot(
            act[:, quarter:], downs_w[2 + h, :, columns], 1, 0
        )

    near_out = give(out_keep, out_send, out_recv, make_out)

    for copy in near_s:
        copy.wait_recv()
    for q in range(2):
        columns = slice(q * quarter, (q + 1) * quarter)
        d_act = dot(grads[:, :half], downs_w[2 * q], 1, 1) + dot(
            grads[:, half:], downs_w[2 * q + 1], 1, 1
        )
        g, u = g_buf[:, columns], u_buf[:, columns]
        sg = jax.nn.sigmoid(g)
        dd[:, columns] = (d_act * u * sg * (1.0 + g * (1.0 - sg))).astype(BF16)
        dd[:, slice((2 + q) * quarter, (3 + q) * quarter)] = (d_act * g * sg).astype(BF16)

    @pl.loop(0, 2)
    def _(t):
        at = pl.multiple_of(t * tile, tile)
        value = dot(act[...], grads[:, pl.ds(pl.multiple_of(half + at, tile), tile)], 0, 0)
        value = value.astype(BF16)
        td[0, :, pl.ds(at, tile)] = value[:quarter]
        td[1, :, pl.ds(at, tile)] = value[quarter:]

    core_d = [send(td.at[q], rd.at[q], core) for q in (1, 0)]
    width_step = 256

    @pl.loop(0, half // width_step)
    def _(t):
        at = pl.multiple_of(t * width_step, width_step)
        value = dot(rows[:, pl.ds(pl.multiple_of(half + at, width_step), width_step)], dd[...], 0, 0)
        value = value.astype(BF16)
        for q in range(2):
            tg[q, pl.ds(at, width_step)] = value[:, q * quarter : (q + 1) * quarter]
            tu[q, pl.ds(at, width_step)] = value[:, (2 + q) * quarter : (3 + q) * quarter]

    core_g = [send(tg.at[q], rg.at[q], core) for q in (1, 0)]
    core_u = [send(tu.at[q], ru.at[q], core) for q in (1, 0)]

    homeward = []
    places = (cap, cap + step, 0, step)

    def finish(keep, arrived, copies, result, which):
        for i in which:
            at = places[i]
            copies[i].wait_recv()
            total = keep[at : at + step].astype(F32) + arrived[at : at + step].astype(F32)
            keep[at : at + step] = total.astype(BF16)
            if at >= cap:
                homeward.append(send(part(keep, at, step), part(result, at, step), home))
            else:
                local(part(keep, at, step), part(result, at, step))

    finish(out_keep, out_recv, near_out, bo, (0, 1))

    for copy in core_d:
        copy.wait_recv()

    @pl.loop(0, 2)
    def _(t):
        at = pl.multiple_of(t * tile, tile)
        value = dot(act[...], grads[:, pl.ds(at, tile)], 0, 0)
        od[:, pl.ds(at, tile)] = (value[:quarter] + rd[0, :, pl.ds(at, tile)].astype(F32)).astype(BF16)
        zsd[:, pl.ds(at, tile)] = (value[quarter:] + rd[1, :, pl.ds(at, tile)].astype(F32)).astype(BF16)

    far_d = send(zsd, zrd, far)

    def make_dx(h, columns):
        value = dot(dd[:, :quarter], gates_w[h, columns], 1, 1)
        value = value + dot(dd[:, quarter : 2 * quarter], gates_w[2 + h, columns], 1, 1)
        value = value + dot(dd[:, 2 * quarter : 3 * quarter], ups_w[h, columns], 1, 1)
        return value + dot(dd[:, 3 * quarter :], ups_w[2 + h, columns], 1, 1)

    near_dx = give(dx_keep, dx_send, dx_recv, make_dx)

    for copy in core_g + core_u:
        copy.wait_recv()

    @pl.loop(0, half // width_step)
    def _(t):
        at = pl.ds(pl.multiple_of(t * width_step, width_step), width_step)
        value = dot(rows[:, at], dd[...], 0, 0)
        for column, got, mine, away in ((0, rg, og, zsg), (2, ru, ou, zsu)):
            first = value[:, column * quarter : (column + 1) * quarter]
            second = value[:, (column + 1) * quarter : (column + 2) * quarter]
            mine[at] = (first + got[0, at].astype(F32)).astype(BF16)
            away[at] = (second + got[1, at].astype(F32)).astype(BF16)

    far_g = send(zsg, zrg, far)
    far_u = send(zsu, zru, far)

    finish(dx_keep, dx_recv, near_dx, bx, (0, 1))
    finish(out_keep, out_recv, near_out, bo, (2, 3))
    finish(dx_keep, dx_recv, near_dx, bx, (2, 3))

    for copy, mine, got in ((far_d, od, zrd), (far_g, og, zrg), (far_u, ou, zru)):
        copy.wait_recv()
        mine[...] = (mine[...].astype(F32) + got[...].astype(F32)).astype(BF16)
    for copy in homeward:
        copy.wait_recv()
    for copy in locals_[len(own_w + own_r):]:
        copy.wait()
    for copy in sent:
        copy.wait_send()


def layer(cap, packed_x, packed_s, wg, wu, wd):
    half, quarter = wg.shape
    slots = 2 * cap
    width = 2 * half
    count = 2 * slots
    vmem = lambda *shape, dtype=BF16: pltpu.VMEM(shape, dtype)
    back = jax.ShapeDtypeStruct((slots, width), BF16)
    like = lambda w: jax.ShapeDtypeStruct(w.shape, BF16)
    anywhere = pl.BlockSpec(memory_space=pl.ANY)
    inside = pl.BlockSpec(memory_space=pltpu.VMEM)
    ff = 2 * quarter
    copies = 43
    return pl.pallas_call(
        functools.partial(layer_kernel, cap, half, quarter),
        out_shape=(back, back, like(wg), like(wu), like(wd)),
        in_specs=[anywhere] * 5,
        out_specs=(anywhere, anywhere, inside, inside, inside),
        scratch_shapes=[
            vmem(count, width), vmem(count, width),
            vmem(4, half, quarter), vmem(4, half, quarter), vmem(4, quarter, half),
            vmem(count, ff, dtype=F32), vmem(count, ff, dtype=F32),
            vmem(count, ff), vmem(count, 2 * ff),
        ]
        + [vmem(slots, width)] * 6
        + [vmem(2, half, quarter), vmem(2, half, quarter), vmem(2, quarter, half)] * 2
        + [vmem(half, quarter), vmem(half, quarter), vmem(quarter, half)] * 2
        + [
            pltpu.SemaphoreType.DMA((copies,)),
            pltpu.SemaphoreType.DMA((copies,)),
            pltpu.SemaphoreType.DMA((16,)),
        ],
        compiler_params=pltpu.CompilerParams(
            collective_id=0, has_side_effects=True, vmem_limit_bytes=60 * 1024 * 1024
        ),
        cost_estimate=pl.CostEstimate(
            flops=18 * count * width * ff, bytes_accessed=40 * half * quarter * 2,
            transcendentals=2 * count * ff,
        ),
    )(packed_x, packed_s, wg, wu, wd)


def layer_by_permutes(experts, capacity, packed_x, packed_s, w_gate, w_up, w_down):
    half, quarter = w_gate.shape
    slots = experts * capacity
    gate_up = jnp.concatenate([w_gate, w_up], axis=1)
    down = w_down
    gate_up_z = swap(gate_up, 4)
    down_z = swap(down, 4)

    def dispatch(packed):
        here = packed[:capacity]
        others = jnp.concatenate(
            [
                swap(packed[d * capacity : (d + 1) * capacity], 8 * d)
                for d in range(1, experts)
            ],
            axis=0,
        )
        return jnp.concatenate([here, others, swap(here, 2), swap(others, 2)], axis=0)

    rows = dispatch(packed_x)
    grads = dispatch(packed_s)

    gate_up_c, down_c = swap(gate_up, 1), swap(down, 1)
    gate_up_zc, down_zc = swap(gate_up_z, 1), swap(down_z, 1)
    w_in = jnp.concatenate(
        [
            jnp.concatenate([gate_up, gate_up_z], axis=1),
            jnp.concatenate([gate_up_c, gate_up_zc], axis=1),
        ],
        axis=0,
    )
    w_out = jnp.concatenate(
        [
            jnp.concatenate([down, down_c], axis=1),
            jnp.concatenate([down_z, down_zc], axis=1),
        ],
        axis=0,
    )

    pre = dot(rows, w_in, 1, 0)
    g = jnp.concatenate([pre[:, :quarter], pre[:, 2 * quarter : 3 * quarter]], axis=1)
    u = jnp.concatenate([pre[:, quarter : 2 * quarter], pre[:, 3 * quarter :]], axis=1)
    sg = jax.nn.sigmoid(g)
    act = (g * sg * u).astype(BF16)

    def give_back(part):
        ready = part[:slots] + swap(part[slots:].astype(BF16), 2).astype(F32)
        ready = ready.astype(BF16)
        return jnp.concatenate(
            [ready[:capacity]]
            + [
                swap(ready[d * capacity : (d + 1) * capacity], 8 * d)
                for d in range(1, experts)
            ],
            axis=0,
        )

    back_out = give_back(dot(act, w_out, 1, 0))
    d_act = dot(grads, w_out, 1, 1)
    d_gate = (d_act * u * sg * (1.0 + g * (1.0 - sg))).astype(BF16)
    d_up = (d_act * g * sg).astype(BF16)
    d_pre = jnp.concatenate(
        [d_gate[:, :quarter], d_up[:, :quarter], d_gate[:, quarter:], d_up[:, quarter:]], axis=1
    )
    back_dx = give_back(dot(d_pre, w_in, 1, 1))

    in_theirs = dot(rows[:, half:], d_pre, 0, 0).astype(BF16)
    out_theirs = dot(act, grads[:, half:], 0, 0).astype(BF16)
    in_mine = dot(rows[:, :half], d_pre, 0, 0) + swap(in_theirs, 1).astype(F32)
    out_mine = dot(act, grads[:, :half], 0, 0) + swap(out_theirs, 1).astype(F32)
    in_sum = in_mine[:, : 2 * quarter] + swap(
        in_mine[:, 2 * quarter :].astype(BF16), 4
    ).astype(F32)
    out_sum = out_mine[:quarter] + swap(out_mine[quarter:].astype(BF16), 4).astype(F32)
    grad_in = in_sum.astype(BF16)
    return back_out, back_dx, grad_in[:, :quarter], grad_in[:, quarter:], out_sum.astype(BF16)


def on_device(tokens, gates, routes, counts, w_gate, w_up, w_down, cotangent):
    peers = lax.axis_size("expert")
    tok_rows, topk = routes.shape
    width = tokens.shape[1]
    half = width // 2
    experts = peers // 8
    capacity = max(2, 3 * tok_rows * topk // (2 * experts))
    flat_n = tok_rows * topk
    slots = experts * capacity
    me = lax.axis_index("expert")
    mine, core = me // 8, me % 2

    valid = jnp.arange(tok_rows, dtype=jnp.int32) < counts[0]
    target = jnp.where(valid[:, None], routes, experts).reshape(flat_n)
    onehot = (target[:, None] == jnp.arange(experts, dtype=jnp.int32)[None, :]).astype(F32)
    earlier = (
        jnp.arange(flat_n)[:, None] > jnp.arange(flat_n)[None, :]
    ).astype(BF16)
    before = dot(earlier, onehot.astype(BF16), 1, 0)
    slot_pos = jnp.sum(before * onehot, axis=1).astype(jnp.int32)
    place = jnp.where(target < experts, (target ^ mine) * capacity + slot_pos, slots)
    put = (place[:, None] == jnp.arange(slots, dtype=jnp.int32)[None, :]).astype(BF16)
    gate_flat = gates.reshape(flat_n)
    if topk == 1:
        tok_flat, cot_flat = tokens, cotangent
    else:
        tok_flat = jnp.repeat(tokens, topk, axis=0)
        cot_flat = jnp.repeat(cotangent, topk, axis=0)
    cot_rows = cot_flat.astype(F32)
    scaled = (gate_flat[:, None] * cot_rows).astype(BF16)

    def own_first(rows):
        return jnp.where(
            core == 0, rows, jnp.concatenate([rows[:, half:], rows[:, :half]], axis=1)
        )

    packed_x = dot(put, own_first(tok_flat), 0, 0).astype(BF16)
    packed_s = dot(put, own_first(scaled), 0, 0).astype(BF16)

    if experts == 2 and capacity % 32 == 0 and half % 256 == 0 and lax.axis_size("groups") == 2:
        back_out, back_dx, grad_wg, grad_wu, grad_wd = layer(
            capacity, packed_x, packed_s, w_gate[0], w_up[0], w_down[0]
        )
    else:
        back_out, back_dx, grad_wg, grad_wu, grad_wd = layer_by_permutes(
            experts, capacity, packed_x, packed_s, w_gate[0], w_up[0], w_down[0]
        )

    out_rows = own_first(dot(put, back_out, 1, 0))
    dx_rows = own_first(dot(put, back_dx, 1, 0))
    mixed = jnp.sum(
        (gate_flat[:, None] * out_rows).reshape(tok_rows, topk, width), axis=1
    ).astype(BF16)
    grad_tokens = jnp.sum(dx_rows.reshape(tok_rows, topk, width), axis=1).astype(BF16)
    grad_gates = jnp.sum(cot_rows * out_rows, axis=1).reshape(tok_rows, topk)
    return (
        mixed,
        grad_tokens,
        grad_gates,
        grad_wg[None],
        grad_wu[None],
        grad_wd[None],
    )


def solution(mesh):
    both, rows = ("groups", "expert"), P(("groups", "expert"), None)
    block = P(both, None, None)
    weight = P("expert", None, None)
    return jax.shard_map(
        on_device,
        mesh=mesh,
        in_specs=(rows, rows, rows, P(both), weight, weight, weight, rows),
        out_specs=(rows, rows, rows, block, block, block),
        check_vma=False,
    )
```
